32 devices in a mesh: grp: 2 (over y), pts: 4 (over z), col: 2 (over x), sub: 2 (over core).
Axes of the slice: x: 2, y: 2, z: 4, core: 2. Of those that a mesh axis runs over, the one named last changes fastest.
Arguments:
- points: bfloat16 [32768, 256], P(('grp', 'pts', 'sub')), parts along dimension 0, may hold values from -12 to 12
- weights: bfloat16 [32768, 128], P(('grp', 'pts', 'sub')), parts along dimension 0, may hold values from -0.046875 to 0.046875
- tile_rows: int32 [4, 8, 128], P(('grp', 'col'), ('pts', 'sub')), parts along dimension 0, may hold values from 0 to 2047, as said below
- tile_count: int32 [4, 8], P(('grp', 'col')), parts along dimension 0, may hold values from 1 to 128, 512 in all within a row
- sketch_pick: int32 [4, 256], P(('grp', 'col')), parts along dimension 0, may hold values from 0 to 511, as said below
- block_targets: bfloat16 [4, 1024, 128], P(('grp', 'col'), ('pts', 'sub')), parts along dimension 0, may hold values from -4 to 4
- core_inv: float32 [1024, 512], P('grp'), parts along dimension 0, as said below
Outputs:
- block_grad: float32 [4, 1024, 128], P(('grp', 'col'), ('pts', 'sub')), parts along dimension 0
- direction: float32 [4, 1024, 128], P(('grp', 'col'), ('pts', 'sub')), parts along dimension 0
The draws below stay inside these ranges and needn't reach their ends.
There are 2 independent parts, one for each index of `grp`. The reference program is written for one: setup_inputs(seed, part) draws one part's arguments, and reference() takes and returns one part's arrays. A program takes and returns all parts, laid end to end along the dimension named above; each array names one. Nothing has to cross between parts.
Inputs may be any that keep to these rules, and one draw needn't show every extreme that they name: For each owner o, the 256 entries tile_rows[:, o, :] are distinct; only slots below tile_count are used. `tile_count`: each row of 8 counts sums to 512, and its largest count is 128. `sketch_pick`: the entries of one row are distinct. `core_inv`: A full-rank matrix.
All inputs are finite; a program needn't handle non-finite values.
Results may differ from the reference program's by a relative error of at most 0.0003.
Values may be sent and summed in bfloat16 or wider, within the bound.
A program may use at most 64 MiB of HBM per device.

```python
import math
import jax
import jax.numpy as jnp
import numpy as np
from jax import lax

DW = 256
OUT = 128
RANK = 512
CAP = 128
PTS_DEV = 2048
OWNERS = 8
TILE = 1024
LIVE = 512
BLOCK = 1024
SKETCH_DEV = 256
NPTS = 16384
N_COL = 2


def draw_points(key, part):
    latent_width = 16
    cluster_total = 8
    base_key = jax.random.fold_in(key, 23)
    center_key, mixing_key, member_key, latent_key, noise_key = jax.random.split(base_key, 5)
    centers = 1.5 * jax.random.normal(center_key, (cluster_total, DW), jnp.float32)
    mixing = jax.random.normal(mixing_key, (latent_width, DW), jnp.float32) / jnp.sqrt(jnp.float32(latent_width))
    member = jax.random.randint(member_key, (NPTS,), 0, cluster_total)
    latent = jax.random.normal(latent_key, (NPTS, latent_width), jnp.float32)
    noise = 0.35 * jax.random.normal(noise_key, (NPTS, DW), jnp.float32)
    onehot = (member[:, None] == jnp.arange(cluster_total)[None, :]).astype(jnp.float32)
    values = jnp.dot(onehot, centers, precision=lax.Precision.HIGHEST)
    values = values + jnp.dot(latent, mixing, precision=lax.Precision.HIGHEST) + noise
    return jnp.clip(values, -12.0, 12.0).astype(jnp.bfloat16)


def draw_tile_rows(key, part):
    owner_keys = jax.random.split(jax.random.fold_in(key, 5), OWNERS)

    def one_owner(owner_key):
        return jax.random.permutation(owner_key, PTS_DEV)[:N_COL * CAP].reshape(N_COL, CAP)
    listed = jax.vmap(one_owner)(owner_keys)
    return jnp.transpose(listed, (1, 0, 2)).astype(jnp.int32)


def draw_sketch_pick(key, part):
    col_keys = jax.random.split(jax.random.fold_in(key, 11), N_COL)

    def one_col(col_key):
        return jax.random.permutation(col_key, LIVE)[:SKETCH_DEV]
    return jax.vmap(one_col)(col_keys).astype(jnp.int32)


def draw_core_inv(key, part):
    diag_key, other_key = jax.random.split(jax.random.fold_in(key, 17))
    diagonal = jax.random.uniform(diag_key, (RANK,), jnp.float32, 1.0, 4.0)
    others = jax.random.normal(other_key, (RANK, RANK), jnp.float32) / jnp.sqrt(jnp.float32(RANK))
    factor = 200.0 / (RANK * jnp.sqrt(jnp.float32(BLOCK)))
    return (factor * (jnp.diag(diagonal) + others)).astype(jnp.float32)


def block_scale(own_key, extent, cuts, low, top_value):
    factor_of, own = 1.0, jax.random.fold_in(own_key, 6)
    for axis_at, shards_of in cuts:
        steps = jnp.exp(jax.random.uniform(jax.random.fold_in(own, axis_at), (shards_of,), jnp.float32, low / len(cuts), top_value / len(cuts)))
        factor_of = factor_of * jnp.repeat(steps, extent[axis_at] // shards_of).reshape([-1 if axis == axis_at else 1 for axis in range(len(extent))])
    return factor_of


def length_profile(number_of, total, bound, lean):
    weights = [(1 << 20) // math.isqrt(standing ** lean) + 1 for standing in range(2, number_of + 1)]
    rest, given = total - bound - (number_of - 1), [1] * (number_of - 1)
    while rest > 0:
        movable = [i for i in range(number_of - 1) if given[i] < bound]
        mass, left = sum([weights[i] for i in movable]), rest
        for i in movable:
            extra = min(bound - given[i], max(1, left * weights[i] // mass), rest)
            given[i] = given[i] + extra
            rest = rest - extra
    return np.array([bound] + given)


def ragged(own_key, count, total, bound, slope):
    if count == 2:
        one = jax.random.randint(own_key, (), max(1, total - bound), min(bound, total - 1) + 1)
        return jnp.stack([one, total - one])
    lengths = jnp.asarray(length_profile(count, total, bound, slope), jnp.int32)
    pairs = (count - 1) // 2
    giver, sink = lengths[1:1 + 2 * pairs:2], lengths[2:2 + 2 * pairs:2]
    slack = jnp.minimum(giver - 1, bound - sink)
    moved = jax.random.randint(jax.random.fold_in(own_key, 1), (pairs,), 0, 1 << 20) % (slack + 1)
    lengths = lengths.at[1:1 + 2 * pairs:2].set(giver - moved).at[2:2 + 2 * pairs:2].set(sink + moved)
    return lengths[jax.random.permutation(jax.random.fold_in(own_key, 2), count)]


def scatter_about(rng, shape, spread, reach, shards=(), held_as=jnp.bfloat16):
    drawn = jax.random.normal(rng, shape, jnp.float32) * spread
    if len(shards) > 0:
        drawn = block_scale(rng, shape, shards, -0.22, 0.18) * drawn
    return jnp.clip(drawn, min=-reach, max=reach).astype(held_as)


def setup_inputs(seed: int = 0, part: int = 0) -> dict:
    splits = jax.random.split(jax.random.key(seed), 8)
    part_keys = jax.random.split(jax.random.fold_in(splits[7], part), 8)
    return {
        "points": draw_points(jax.random.fold_in(jax.random.fold_in(splits[7], part), 71), part),
        "weights": scatter_about(part_keys[1], (NPTS, OUT), NPTS ** -0.5, 0.046875, ((0, 8),)),
        "tile_rows": draw_tile_rows(jax.random.fold_in(jax.random.fold_in(splits[7], part), 71), part),
        "tile_count": jax.vmap(lambda own: ragged(own, OWNERS, LIVE, CAP, 2))(jax.random.split(part_keys[3], N_COL)).reshape((N_COL, OWNERS)).astype(jnp.int32),
        "sketch_pick": draw_sketch_pick(jax.random.fold_in(jax.random.fold_in(splits[7], part), 71), part),
        "block_targets": scatter_about(part_keys[5], (N_COL, TILE, OUT), 0.5, 4.0, ((0, 2), (1, 8))),
        "core_inv": draw_core_inv(jax.random.fold_in(jax.random.fold_in(splits[7], part), 71), part),
    }


RIDGE_COEF = 50.0
HIGHEST_PREC = lax.Precision.HIGHEST


def sq_norms(values):
    widened = values.astype(jnp.float32)
    return jnp.sum(widened * widened, axis=1)


def kernel(left_x, right_x):
    inner_prods = jnp.dot(left_x.astype(jnp.float32), right_x.astype(jnp.float32).T, precision=HIGHEST_PREC)
    dist_sq = sq_norms(left_x)[:, None] + sq_norms(right_x)[None, :] - 2.0 * inner_prods
    return jnp.exp(-dist_sq / DW)


def live_slots(counts):
    offsets = jnp.cumsum(counts) - counts
    rank_ids = jnp.arange(LIVE, dtype=jnp.int32)
    owner_of = jnp.sum((offsets[None, :] <= rank_ids[:, None]).astype(jnp.int32), axis=1) - 1
    return (owner_of * CAP + rank_ids - jnp.take(offsets, owner_of)).astype(jnp.int32)


def reference(points, weights, tile_rows, tile_count, sketch_pick, block_targets, core_inv):
    owner_base = (jnp.arange(OWNERS, dtype=jnp.int32) * PTS_DEV)[None, :, None]
    global_rows = (tile_rows + owner_base).reshape(N_COL, TILE).astype(jnp.int32)
    live_slot = jax.vmap(live_slots)(tile_count)
    live_rows = jnp.take_along_axis(global_rows, live_slot, axis=1).reshape(-1)
    live_x = jnp.take(points, live_rows, axis=0)
    all_sq = sq_norms(points)
    wide_points = points.astype(jnp.float32)
    wide_weights = weights.astype(jnp.float32)

    def rows_term(row_block):
        inner_prods = jnp.dot(row_block.astype(jnp.float32), wide_points.T, precision=HIGHEST_PREC)
        dist_sq = sq_norms(row_block)[:, None] + all_sq[None, :] - 2.0 * inner_prods
        kern_vals = jnp.exp(-dist_sq / DW)
        return jnp.dot(kern_vals, wide_weights, precision=HIGHEST_PREC)

    row_step = math.gcd(BLOCK, 512)
    part_live = lax.map(rows_term, live_x.reshape(BLOCK // row_step, row_step, DW)).reshape(N_COL, LIVE, OUT)
    offsets = jnp.cumsum(tile_count, axis=1) - tile_count
    slot_ids = jnp.arange(CAP, dtype=jnp.int32)
    used_mask = slot_ids[None, None, :] < tile_count[:, :, None]
    rank_of = jnp.minimum(offsets[:, :, None] + slot_ids[None, None, :], LIVE - 1).reshape(N_COL, TILE).astype(jnp.int32)
    slab_sum = jnp.take_along_axis(part_live, rank_of[:, :, None], axis=1)
    used_float = used_mask.reshape(N_COL, TILE, 1).astype(jnp.float32)
    alpha_block = jnp.take(weights, global_rows.reshape(-1), axis=0).astype(jnp.float32).reshape(N_COL, TILE, OUT)
    block_grad = used_float * (slab_sum + RIDGE_COEF * alpha_block - block_targets.astype(jnp.float32))
    sketch_slot = jnp.take_along_axis(live_slot, sketch_pick, axis=1)
    sketch_rows = jnp.take_along_axis(global_rows, sketch_slot, axis=1).reshape(-1)
    sketch_x = jnp.take(points, sketch_rows, axis=0)
    block_x = jnp.take(points, global_rows.reshape(-1), axis=0)
    flat_used = used_float.reshape(-1, 1)
    sketch_kern = kernel(block_x, sketch_x) * flat_used
    flat_grad = block_grad.reshape(-1, OUT)
    projected = jnp.dot(sketch_kern.T, flat_grad, precision=HIGHEST_PREC)
    weighted = jnp.dot(core_inv, projected, precision=HIGHEST_PREC)
    direction = flat_used * (flat_grad - jnp.dot(sketch_kern, weighted, precision=HIGHEST_PREC))
    return block_grad, direction.reshape(N_COL, TILE, OUT)
```

```python
import functools
import math

import jax
import jax.numpy as jnp
from jax import lax
from jax.experimental import pallas as pl
from jax.experimental.pallas import tpu as pltpu
from jax.sharding import PartitionSpec as P

RIDGE_COEF = 50.0
MESH = pl.DeviceIdType.MESH
F32 = jnp.float32
BF16 = jnp.bfloat16
NN = (((1,), (0,)), ((), ()))
NT = (((1,), (1,)), ((), ()))


def mm(left, right, dims=NN):
    return lax.dot_general(left, right, dims, preferred_element_type=F32)


def split2(value):
    high = value.astype(BF16)
    return high, (value - high.astype(F32)).astype(BF16)


def mm3(left, right, dims=NN):
    (lh, ll), (rh, rl) = left, right
    return mm(lh, rh, dims) + (mm(lh, rl, dims) + mm(ll, rh, dims))


def mix(index, step, total):
    if total & (total - 1):
        return (index + step) % total
    out, bit = 0, 1
    while bit < total:
        out = out + bit * (((index // bit) % 2 + (step // bit) % 2) % 2)
        bit *= 2
    return out


def each(low, high, body):
    if high - low <= 8:
        for i in range(low, high):
            body(i)
    elif high > low:
        lax.fori_loop(low, high, lambda i, c: (body(i), c)[1], 0)


def sq_col(x):
    wide = x.astype(F32)
    return jnp.sum(wide * wide, axis=1, keepdims=True)


def sq_row(x):
    wide = x.astype(F32)
    high, low = split2(wide * wide)
    ones = jnp.ones((8, x.shape[1]), BF16)
    return (mm(ones, high, NT) + mm(ones, low, NT))[0:1, :]


def column(row):
    return jnp.transpose(jnp.broadcast_to(row, (8, row.shape[1])))[:, 0:1]


def body(
    sizes, cnt_ref, rows_ref, pick_ref, targ_ref, points_hbm, weights_hbm, core_hbm,
    bg_ref, dir_ref,
    pts_v, wts_v, core_v, psq, core_hi, core_lo,
    xbuf, part, subr, lsum, lrec, skx, kern, pj, pjr, psum, prec, fbuf,
    in_sem, ag_s, ag_r, fw_s, fw_r, sb_s, sb_r, ln_s, ln_r, sk_s, sk_r,
    pe_s, pe_r, rs_s, rs_r, fa_s, fa_r, ff_s, ff_r,
):
    n_p, n_c, n_s, cap, width, outs, n_pts, n_sk, rank, piece = sizes
    n_q = n_p * n_c
    half = rank // n_s
    owners = n_p * n_s
    p = lax.axis_index("pts")
    c = lax.axis_index("col")
    s = lax.axis_index("sub")
    q = p * n_c + c
    other = 1 - s
    sibling = {"sub": other}
    c2 = math.log2(math.e) / width

    def at_q(k):
        peer = mix(q, k, n_q)
        return peer, {"pts": peer // n_c, "col": peer % n_c}

    def rc(src, dst, ssem, rsem, dev):
        return pltpu.make_async_remote_copy(
            src_ref=src, dst_ref=dst, send_sem=ssem, recv_sem=rsem,
            device_id=dev, device_id_type=MESH,
        )

    in_pts = pltpu.make_async_copy(points_hbm, pts_v, in_sem.at[0])
    in_wts = pltpu.make_async_copy(weights_hbm, wts_v, in_sem.at[1])
    in_core = pltpu.make_async_copy(core_hbm, core_v, in_sem.at[2])
    in_pts.start()
    in_wts.start()
    in_core.start()

    barrier = pltpu.get_barrier_semaphore()
    pl.semaphore_signal(barrier, inc=1, device_id=sibling, device_id_type=MESH)

    def greet(k):
        pl.semaphore_signal(barrier, inc=1, device_id=at_q(k)[1], device_id_type=MESH)

    each(1, n_q, greet)

    own_count = cnt_ref[0, p * n_s + s]
    used = lax.broadcasted_iota(jnp.int32, (cap, 1), 0) < own_count
    rows = jnp.where(used, column(rows_ref[0].astype(F32)), -1.0)
    ids = lax.broadcasted_iota(jnp.int32, (1, n_pts), 1).astype(F32)
    pick_rows = jnp.where(rows == ids, 1.0, 0.0).astype(BF16)
    in_pts.wait()
    xbuf[p, s] = mm(pick_rows, pts_v[...]).astype(BF16)
    pl.semaphore_wait(barrier, n_q)

    def fw(pk, slot):
        return rc(xbuf.at[pk, slot], xbuf.at[pk, slot], fw_s.at[pk], fw_r.at[pk], sibling)

    fw(p, s).start()

    def ag_send(k):
        peer = mix(p, k, n_p)
        rc(xbuf.at[p, s], xbuf.at[p, s], ag_s.at[peer], ag_r.at[p], {"pts": peer}).start()

    each(1, n_p, ag_send)

    in_wts.wait()
    alpha = mm(pick_rows, wts_v[...])
    psq[...] = sq_row(pts_v[...]) * c2

    def lane_forward(k):
        pk = mix(p, k, n_p)
        rc(xbuf.at[pk, s], xbuf.at[pk, s], ag_s.at[pk], ag_r.at[pk], {"pts": pk}).wait_recv()
        fw(pk, s).start()

    step = math.gcd(n_pts, 512)

    def compute(k):
        pk = mix(p, k, n_p)
        fw(pk, other).wait_recv()
        x = xbuf[pk].reshape(n_s * cap, width)
        left = sq_col(x) * c2

        def add(i, acc):
            at = pl.ds(pl.multiple_of(i * step, step), step)
            inner = mm(x, pts_v[at, :], NT)
            vals = jnp.exp2((inner * (2.0 * c2) - left) - psq[:, at])
            high, low = split2(vals)
            w = wts_v[at, :]
            return acc + (mm(high, w) + mm(low, w))

        acc = lax.fori_loop(0, n_pts // step, add, jnp.zeros((n_s * cap, outs), F32))
        part[pk] = acc.reshape(n_s, cap, outs)
        rc(part.at[pk, other], subr.at[pk], sb_s.at[pk], sb_r.at[pk], sibling).start()

    def sub_wait(pk):
        rc(part.at[pk, other], subr.at[pk], sb_s.at[pk], sb_r.at[pk], sibling).wait_recv()

    def lane_send(k):
        pk = mix(p, k, n_p)
        sub_wait(pk)
        lsum[pk] = part[pk, s] + subr[pk]
        rc(lsum.at[pk], lrec.at[p], ln_s.at[pk], ln_r.at[p], {"pts": pk}).start()

    compute(0)
    if n_p > 1:
        lane_forward(1)

        def stage(k):
            lane_forward(k + 1)
            compute(k)

            @pl.when(k >= 2)
            def _():
                lane_send(k - 1)

        if n_p <= 4:
            for k in range(1, n_p - 1):
                lane_forward(k + 1)
                compute(k)
                if k >= 2:
                    lane_send(k - 1)
        else:
            lax.fori_loop(1, n_p - 1, lambda k, z: (stage(k), z)[1], 0)
        compute(n_p - 1)
        if n_p > 2:
            lane_send(n_p - 2)

    slot = lax.broadcasted_iota(jnp.int32, (1, owners * cap), 1)
    rank_of = jnp.full((1, owners * cap), -1, jnp.int32)
    before = 0
    for o in range(owners):
        have = cnt_ref[0, o]
        local = slot - o * cap
        rank_of = jnp.where((local >= 0) & (local < have), local + before, rank_of)
        before = before + have
    picks = column(pick_ref[...].astype(F32))
    onehot = jnp.where(picks == rank_of.astype(F32), 1.0, 0.0).astype(BF16)
    skx[c] = mm(onehot, xbuf[...].reshape(owners * cap, width)).astype(BF16)

    def sk(ck, mine):
        return rc(skx.at[mine], skx.at[mine], sk_s.at[ck], sk_r.at[mine], {"col": ck})

    each(1, n_c, lambda k: sk(mix(c, k, n_c), c).start())
    if n_p > 1:
        lane_send(n_p - 1)

    in_core.wait()
    high, low = split2(core_v[...])
    core_hi[...] = high
    core_lo[...] = low

    each(1, n_c, lambda k: sk(mix(c, k, n_c), mix(c, k, n_c)).wait_recv())
    own_x = xbuf[p, s]
    sketch = skx[...].reshape(rank, width)
    kern_t = jnp.exp2((mm(sketch, own_x, NT) * (2.0 * c2) - sq_col(sketch) * c2) - sq_row(own_x) * c2)
    kern_t = split2(kern_t)
    kern[...] = jnp.exp2((mm(own_x, sketch, NT) * (2.0 * c2) - sq_col(own_x) * c2) - sq_row(sketch) * c2)

    sub_wait(p)
    slab = part[p, s] + subr[p]
    for k in range(1, n_p):
        pk = mix(p, k, n_p)
        rc(lsum.at[pk], lrec.at[pk], ln_s.at[pk], ln_r.at[pk], {"pts": pk}).wait_recv()
        slab = slab + lrec[pk]
    used_f = used.astype(F32)
    grad = used_f * (slab + RIDGE_COEF * alpha - targ_ref[0].astype(F32))
    bg_ref[0] = grad

    proj = mm3(kern_t, split2(grad))
    if half < n_q * piece:
        pj[...] = jnp.zeros_like(pj)
    for h in range(n_s):
        pj[h, 0:half, :] = proj[h * half:(h + 1) * half, :]
    pe = rc(pj.at[other], pjr, pe_s, pe_r, sibling)
    pe.start()
    pe.wait_recv()
    psum[...] = (pj[s] + pjr[...]).reshape(n_q, piece, outs)

    def rs(k, mine):
        peer, dev = at_q(k)
        return rc(psum.at[peer], prec.at[mine(peer)], rs_s.at[peer], rs_r.at[mine(peer)], dev)

    each(1, n_q, lambda k: rs(k, lambda peer: q).start())
    total = psum[q]
    if n_q <= 8:
        for k in range(1, n_q):
            rs(k, lambda peer: peer).wait_recv()
            total = total + prec[mix(q, k, n_q)]
    else:
        def gain(k, run):
            rs(k, lambda peer: peer).wait_recv()
            return run + prec[mix(q, k, n_q)]

        total = lax.fori_loop(1, n_q, gain, total)
    fbuf[s, q] = total

    def fa(k, mine):
        peer, dev = at_q(k)
        at = fbuf.at[s, mine(peer)]
        return rc(at, at, fa_s.at[peer], fa_r.at[mine(peer)], dev)

    def ff(peer, side):
        at = fbuf.at[side, peer]
        return rc(at, at, ff_s.at[peer], ff_r.at[peer], sibling)

    each(1, n_q, lambda k: fa(k, lambda peer: q).start())
    ff(q, s).start()

    def relay(k):
        fa(k, lambda peer: peer).wait_recv()
        ff(mix(q, k, n_q), s).start()

    each(1, n_q, relay)
    each(0, n_q, lambda k: ff(mix(q, k, n_q), other).wait_recv())

    weighted = jnp.zeros((rank, outs), F32)
    for h in range(n_s):
        block = fbuf[h].reshape(n_q * piece, outs)[0:half, :]
        cols = slice(h * half, (h + 1) * half)
        weighted = weighted + mm3((core_hi[:, cols], core_lo[:, cols]), split2(block))
    dir_ref[0] = used_f * (grad - mm3(split2(kern[...]), split2(weighted)))

    def lane_done(k):
        pk = mix(p, k, n_p)
        rc(xbuf.at[p, s], xbuf.at[p, s], ag_s.at[pk], ag_r.at[p], {"pts": pk}).wait_send()
        rc(lsum.at[pk], lrec.at[p], ln_s.at[pk], ln_r.at[p], {"pts": pk}).wait_send()

    def chip_done(k):
        pk = mix(p, k, n_p)
        fw(pk, s).wait_send()
        rc(part.at[pk, other], subr.at[pk], sb_s.at[pk], sb_r.at[pk], sibling).wait_send()

    def piece_done(k):
        rs(k, lambda peer: q).wait_send()
        fa(k, lambda peer: q).wait_send()

    each(1, n_p, lane_done)
    each(0, n_p, chip_done)
    each(1, n_c, lambda k: sk(mix(c, k, n_c), c).wait_send())
    pe.wait_send()
    each(1, n_q, piece_done)
    each(0, n_q, lambda k: ff(mix(q, k, n_q), s).wait_send())


def per_device(mesh_sizes, points, weights, tile_rows, tile_count, sketch_pick, block_targets, core_inv):
    n_p, n_c, n_s = mesh_sizes
    cap = tile_rows.shape[2]
    n_pts, width = points.shape
    outs = weights.shape[1]
    n_sk = sketch_pick.shape[1]
    rank = core_inv.shape[0]
    n_q = n_p * n_c
    piece = max(8, -(-rank // (n_s * n_q)))
    sizes = (n_p, n_c, n_s, cap, width, outs, n_pts, n_sk, rank, piece)
    vmem = pl.BlockSpec(memory_space=pltpu.VMEM)
    smem = pl.BlockSpec(memory_space=pltpu.SMEM)
    hbm = pl.BlockSpec(memory_space=pl.ANY)
    dma = pltpu.SemaphoreType.DMA
    out = jax.ShapeDtypeStruct((1, cap, outs), F32)
    return pl.pallas_call(
        functools.partial(body, sizes),
        out_shape=(out, out),
        in_specs=[smem, vmem, vmem, vmem, hbm, hbm, hbm],
        out_specs=(vmem, vmem),
        scratch_shapes=[
            pltpu.VMEM((n_pts, width), BF16),
            pltpu.VMEM((n_pts, outs), BF16),
            pltpu.VMEM((rank, rank), F32),
            pltpu.VMEM((1, n_pts), F32),
            pltpu.VMEM((rank, rank), BF16),
            pltpu.VMEM((rank, rank), BF16),
            pltpu.VMEM((n_p, n_s, cap, width), BF16),
            pltpu.VMEM((n_p, n_s, cap, outs), F32),
            pltpu.VMEM((n_p, cap, outs), F32),
            pltpu.VMEM((n_p, cap, outs), F32),
            pltpu.VMEM((n_p, cap, outs), F32),
            pltpu.VMEM((n_c, n_sk, width), BF16),
            pltpu.VMEM((cap, rank), F32),
            pltpu.VMEM((n_s, n_q * piece, outs), F32),
            pltpu.VMEM((n_q * piece, outs), F32),
            pltpu.VMEM((n_q, piece, outs), F32),
            pltpu.VMEM((n_q, piece, outs), F32),
            pltpu.VMEM((n_s, n_q, piece, outs), F32),
            dma((3,)),
            dma((n_p,)), dma((n_p,)),
            dma((n_p,)), dma((n_p,)),
            dma((n_p,)), dma((n_p,)),
            dma((n_p,)), dma((n_p,)),
            dma((n_c,)), dma((n_c,)),
            dma(()), dma(()),
            dma((n_q,)), dma((n_q,)),
            dma((n_q,)), dma((n_q,)),
            dma((n_q,)), dma((n_q,)),
        ],
        compiler_params=pltpu.CompilerParams(
            collective_id=0, has_side_effects=True, vmem_limit_bytes=48 * 1024 * 1024
        ),
    )(tile_count, tile_rows, sketch_pick, block_targets, points, weights, core_inv)


def solution(mesh):
    in_specs = (
        P(("grp", "pts", "sub"), None),
        P(("grp", "pts", "sub"), None),
        P(("grp", "col"), ("pts", "sub"), None),
        P(("grp", "col"), None),
        P(("grp", "col"), None),
        P(("grp", "col"), ("pts", "sub"), None),
        P("grp", None),
    )
    out_specs = (P(("grp", "col"), ("pts", "sub"), None), P(("grp", "col"), ("pts", "sub"), None))
    mesh_sizes = (mesh.shape["pts"], mesh.shape["col"], mesh.shape["sub"])
    return jax.shard_map(
        functools.partial(per_device, mesh_sizes), mesh=mesh, in_specs=in_specs,
        out_specs=out_specs, check_vma=False,
    )
```

```python
import functools
import math

import jax
import jax.numpy as jnp
from jax import lax
from jax.experimental import pallas as pl
from jax.experimental.pallas import tpu as pltpu
from jax.sharding import PartitionSpec as P

RIDGE_COEF = 50.0
MESH = pl.DeviceIdType.MESH
F32 = jnp.float32
BF16 = jnp.bfloat16
NN = (((1,), (0,)), ((), ()))
NT = (((1,), (1,)), ((), ()))


def mm(left, right, dims=NN):
    return lax.dot_general(left, right, dims, preferred_element_type=F32)


def split2(value):
    high = value.astype(BF16)
    return high, (value - high.astype(F32)).astype(BF16)


def mm3(left, right, dims=NN):
    (lh, ll), (rh, rl) = left, right
    return mm(lh, rh, dims) + (mm(lh, rl, dims) + mm(ll, rh, dims))


def mix(index, step, total):
    if total & (total - 1):
        return (index + step) % total
    out, bit = 0, 1
    while bit < total:
        out = out + bit * (((index // bit) % 2 + (step // bit) % 2) % 2)
        bit *= 2
    return out


def each(low, high, body):
    if high - low <= 8:
        for i in range(low, high):
            body(i)
    elif high > low:
        lax.fori_loop(low, high, lambda i, c: (body(i), c)[1], 0)


def sq_col(x):
    wide = x.astype(F32)
    return jnp.sum(wide * wide, axis=1, keepdims=True)


def sq_row(x):
    wide = x.astype(F32)
    high, low = split2(wide * wide)
    ones = jnp.ones((8, x.shape[1]), BF16)
    return (mm(ones, high, NT) + mm(ones, low, NT))[0:1, :]


def column(row):
    return jnp.transpose(jnp.broadcast_to(row, (8, row.shape[1])))[:, 0:1]


def body(
    sizes, cnt_hbm, rows_hbm, pick_hbm, targ_hbm, points_hbm, weights_hbm, core_hbm,
    slab_ref, rest_ref, fix_ref,
    cnt_ref, rows_ref, pick_ref, targ_ref,
    pts_v, wts_v, core_v, psq, core_hi, core_lo,
    xbuf, part, subr, lsum, lrec, skx, out_hi, out_lo, pj, pjr, psum, prec, fbuf,
    in_sem, ag_s, ag_r, fw_s, fw_r, sb_s, sb_r, ln_s, ln_r, sk_s, sk_r,
    pe_s, pe_r, rs_s, rs_r, fa_s, fa_r, ff_s, ff_r,
):
    n_p, n_c, n_s, cap, width, outs, n_pts, n_sk, rank, piece = sizes
    n_q = n_p * n_c
    half = rank // n_s
    owners = n_p * n_s
    p = lax.axis_index("pts")
    c = lax.axis_index("col")
    s = lax.axis_index("sub")
    q = p * n_c + c
    other = 1 - s
    sibling = {"sub": other}
    c2 = math.log2(math.e) / width

    def at_q(k):
        peer = mix(q, k, n_q)
        return peer, {"pts": peer // n_c, "col": peer % n_c}

    def rc(src, dst, ssem, rsem, dev):
        return pltpu.make_async_remote_copy(
            src_ref=src, dst_ref=dst, send_sem=ssem, recv_sem=rsem,
            device_id=dev, device_id_type=MESH,
        )

    loads = [
        pltpu.make_async_copy(src, dst, in_sem.at[i])
        for i, (src, dst) in enumerate((
            (cnt_hbm, cnt_ref), (rows_hbm, rows_ref), (points_hbm, pts_v), (weights_hbm, wts_v),
            (pick_hbm, pick_ref), (targ_hbm, targ_ref), (core_hbm, core_v),
        ))
    ]
    for load in loads:
        load.start()
    in_cnt, in_rows, in_pts, in_wts, in_pick, in_targ, in_core = loads

    barrier = pltpu.get_barrier_semaphore()
    pl.semaphore_signal(barrier, inc=1, device_id=sibling, device_id_type=MESH)

    def greet(k):
        pl.semaphore_signal(barrier, inc=1, device_id=at_q(k)[1], device_id_type=MESH)

    each(1, n_q, greet)

    in_cnt.wait()
    in_rows.wait()
    own_count = cnt_ref[0, p * n_s + s]
    used = lax.broadcasted_iota(jnp.int32, (cap, 1), 0) < own_count
    rows = jnp.where(used, column(rows_ref[0].astype(F32)), -1.0)
    ids = lax.broadcasted_iota(jnp.int32, (1, n_pts), 1).astype(F32)
    pick_rows = jnp.where(rows == ids, 1.0, 0.0).astype(BF16)
    in_pts.wait()
    xbuf[p, s] = mm(pick_rows, pts_v[...]).astype(BF16)
    pl.semaphore_wait(barrier, n_q)

    def fw(pk, slot):
        return rc(xbuf.at[pk, slot], xbuf.at[pk, slot], fw_s.at[pk], fw_r.at[pk], sibling)

    fw(p, s).start()

    def ag_send(k):
        peer = mix(p, k, n_p)
        rc(xbuf.at[p, s], xbuf.at[p, s], ag_s.at[peer], ag_r.at[p], {"pts": peer}).start()

    each(1, n_p, ag_send)

    in_wts.wait()
    alpha = mm(pick_rows, wts_v[...])
    psq[...] = sq_row(pts_v[...]) * c2

    def lane_forward(k):
        pk = mix(p, k, n_p)
        rc(xbuf.at[pk, s], xbuf.at[pk, s], ag_s.at[pk], ag_r.at[pk], {"pts": pk}).wait_recv()
        fw(pk, s).start()

    step = math.gcd(n_pts, 512)

    def compute(k):
        pk = mix(p, k, n_p)
        fw(pk, other).wait_recv()
        x = xbuf[pk].reshape(n_s * cap, width)
        left = sq_col(x) * c2

        acc = jnp.zeros((n_s * cap, outs), F32)
        for i in range(n_pts // step):
            at = slice(i * step, (i + 1) * step)
            inner = mm(x, pts_v[at, :], NT)
            vals = jnp.exp2((inner * (2.0 * c2) - left) - psq[:, at])
            high, low = split2(vals)
            w = wts_v[at, :]
            acc = acc + (mm(high, w) + mm(low, w))
        part[pk] = acc.reshape(n_s, cap, outs)
        rc(part.at[pk, other], subr.at[pk], sb_s.at[pk], sb_r.at[pk], sibling).start()

    def sub_wait(pk):
        rc(part.at[pk, other], subr.at[pk], sb_s.at[pk], sb_r.at[pk], sibling).wait_recv()

    def lane_send(k):
        pk = mix(p, k, n_p)
        sub_wait(pk)
        lsum[pk] = part[pk, s] + subr[pk]
        rc(lsum.at[pk], lrec.at[p], ln_s.at[pk], ln_r.at[p], {"pts": pk}).start()

    compute(0)
    if n_p > 1:
        lane_forward(1)

        def stage(k):
            lane_forward(k + 1)
            compute(k)

            @pl.when(k >= 2)
            def _():
                lane_send(k - 1)

        if n_p <= 4:
            for k in range(1, n_p - 1):
                lane_forward(k + 1)
                compute(k)
                if k >= 2:
                    lane_send(k - 1)
        else:
            lax.fori_loop(1, n_p - 1, lambda k, z: (stage(k), z)[1], 0)
        compute(n_p - 1)
        if n_p > 2:
            lane_send(n_p - 2)

    slot = lax.broadcasted_iota(jnp.int32, (1, owners * cap), 1)
    rank_of = jnp.full((1, owners * cap), -1, jnp.int32)
    before = 0
    for o in range(owners):
        have = cnt_ref[0, o]
        local = slot - o * cap
        rank_of = jnp.where((local >= 0) & (local < have), local + before, rank_of)
        before = before + have
    in_pick.wait()
    picks = column(pick_ref[...].astype(F32))
    onehot = jnp.where(picks == rank_of.astype(F32), 1.0, 0.0).astype(BF16)
    skx[c] = mm(onehot, xbuf[...].reshape(owners * cap, width)).astype(BF16)

    def sk(ck, mine):
        return rc(skx.at[mine], skx.at[mine], sk_s.at[ck], sk_r.at[mine], {"col": ck})

    each(1, n_c, lambda k: sk(mix(c, k, n_c), c).start())
    if n_p > 1:
        lane_send(n_p - 1)

    in_core.wait()
    high, low = split2(core_v[...])
    core_hi[...] = high
    core_lo[...] = low

    each(1, n_c, lambda k: sk(mix(c, k, n_c), mix(c, k, n_c)).wait_recv())
    own_x = xbuf[p, s]
    sketch = skx[...].reshape(rank, width)
    kern_t = jnp.exp2((mm(sketch, own_x, NT) * (2.0 * c2) - sq_col(sketch) * c2) - sq_row(own_x) * c2)
    kern_t = split2(kern_t)
    kern = jnp.exp2((mm(own_x, sketch, NT) * (2.0 * c2) - sq_col(own_x) * c2) - sq_row(sketch) * c2)
    high, low = split2(mm3(split2(kern), (core_hi[...], core_lo[...])))
    out_hi[...] = high
    out_lo[...] = low

    sub_wait(p)
    slab = part[p, s] + subr[p]
    for k in range(1, n_p):
        pk = mix(p, k, n_p)
        rc(lsum.at[pk], lrec.at[pk], ln_s.at[pk], ln_r.at[pk], {"pts": pk}).wait_recv()
        slab = slab + lrec[pk]
    in_targ.wait()
    used_f = used.astype(F32)
    rest = used_f * (RIDGE_COEF * alpha - targ_ref[0].astype(F32))
    slab = used_f * slab
    slab_ref[0] = slab
    rest_ref[0] = rest
    grad = slab + rest

    proj = mm3(kern_t, split2(grad))
    if half < n_q * piece:
        pj[...] = jnp.zeros_like(pj)
    for h in range(n_s):
        pj[h, 0:half, :] = proj[h * half:(h + 1) * half, :]
    pe = rc(pj.at[other], pjr, pe_s, pe_r, sibling)
    pe.start()
    pe.wait_recv()
    psum[...] = (pj[s] + pjr[...]).reshape(n_q, piece, outs)

    def rs(k, mine):
        peer, dev = at_q(k)
        return rc(psum.at[peer], prec.at[mine(peer)], rs_s.at[peer], rs_r.at[mine(peer)], dev)

    each(1, n_q, lambda k: rs(k, lambda peer: q).start())
    total = psum[q]
    if n_q <= 8:
        for k in range(1, n_q):
            rs(k, lambda peer: peer).wait_recv()
            total = total + prec[mix(q, k, n_q)]
    else:
        def gain(k, run):
            rs(k, lambda peer: peer).wait_recv()
            return run + prec[mix(q, k, n_q)]

        total = lax.fori_loop(1, n_q, gain, total)
    fbuf[s, q] = total

    def fa(k, mine):
        peer, dev = at_q(k)
        at = fbuf.at[s, mine(peer)]
        return rc(at, at, fa_s.at[peer], fa_r.at[mine(peer)], dev)

    def ff(peer, side):
        at = fbuf.at[side, peer]
        return rc(at, at, ff_s.at[peer], ff_r.at[peer], sibling)

    each(1, n_q, lambda k: fa(k, lambda peer: q).start())
    ff(q, s).start()

    def relay(k):
        fa(k, lambda peer: peer).wait_recv()
        ff(mix(q, k, n_q), s).start()

    each(1, n_q, relay)

    def correct(h):
        block = fbuf[h].reshape(n_q * piece, outs)[0:half, :]
        cols = pl.ds(pl.multiple_of(h * half, half), half)
        return mm3((out_hi[:, cols], out_lo[:, cols]), split2(block))

    fix = correct(s)
    each(0, n_q, lambda k: ff(mix(q, k, n_q), other).wait_recv())
    fix_ref[0] = used_f * (fix + correct(other))

    def lane_done(k):
        pk = mix(p, k, n_p)
        rc(xbuf.at[p, s], xbuf.at[p, s], ag_s.at[pk], ag_r.at[p], {"pts": pk}).wait_send()
        rc(lsum.at[pk], lrec.at[p], ln_s.at[pk], ln_r.at[p], {"pts": pk}).wait_send()

    def chip_done(k):
        pk = mix(p, k, n_p)
        fw(pk, s).wait_send()
        rc(part.at[pk, other], subr.at[pk], sb_s.at[pk], sb_r.at[pk], sibling).wait_send()

    def piece_done(k):
        rs(k, lambda peer: q).wait_send()
        fa(k, lambda peer: q).wait_send()

    each(1, n_p, lane_done)
    each(0, n_p, chip_done)
    each(1, n_c, lambda k: sk(mix(c, k, n_c), c).wait_send())
    pe.wait_send()
    each(1, n_q, piece_done)
    each(0, n_q, lambda k: ff(mix(q, k, n_q), s).wait_send())


def per_device(mesh_sizes, points, weights, tile_rows, tile_count, sketch_pick, block_targets, core_inv):
    n_p, n_c, n_s = mesh_sizes
    cap = tile_rows.shape[2]
    n_pts, width = points.shape
    outs = weights.shape[1]
    n_sk = sketch_pick.shape[1]
    rank = core_inv.shape[0]
    n_q = n_p * n_c
    piece = max(8, -(-rank // (n_s * n_q)))
    sizes = (n_p, n_c, n_s, cap, width, outs, n_pts, n_sk, rank, piece)
    vmem = pl.BlockSpec(memory_space=pltpu.VMEM)
    hbm = pl.BlockSpec(memory_space=pl.ANY)
    dma = pltpu.SemaphoreType.DMA
    out = jax.ShapeDtypeStruct((1, cap, outs), F32)
    slab, rest, fix = pl.pallas_call(
        functools.partial(body, sizes),
        out_shape=(out, out, out),
        in_specs=[hbm] * 7,
        out_specs=(vmem, vmem, vmem),
        scratch_shapes=[
            pltpu.SMEM(tile_count.shape, jnp.int32),
            pltpu.VMEM(tile_rows.shape, jnp.int32),
            pltpu.VMEM(sketch_pick.shape, jnp.int32),
            pltpu.VMEM(block_targets.shape, BF16),
            pltpu.VMEM((n_pts, width), BF16),
            pltpu.VMEM((n_pts, outs), BF16),
            pltpu.VMEM((rank, rank), F32),
            pltpu.VMEM((1, n_pts), F32),
            pltpu.VMEM((rank, rank), BF16),
            pltpu.VMEM((rank, rank), BF16),
            pltpu.VMEM((n_p, n_s, cap, width), BF16),
            pltpu.VMEM((n_p, n_s, cap, outs), F32),
            pltpu.VMEM((n_p, cap, outs), F32),
            pltpu.VMEM((n_p, cap, outs), F32),
            pltpu.VMEM((n_p, cap, outs), F32),
            pltpu.VMEM((n_c, n_sk, width), BF16),
            pltpu.VMEM((cap, rank), BF16),
            pltpu.VMEM((cap, rank), BF16),
            pltpu.VMEM((n_s, n_q * piece, outs), F32),
            pltpu.VMEM((n_q * piece, outs), F32),
            pltpu.VMEM((n_q, piece, outs), F32),
            pltpu.VMEM((n_q, piece, outs), F32),
            pltpu.VMEM((n_s, n_q, piece, outs), F32),
            dma((7,)),
            dma((n_p,)), dma((n_p,)),
            dma((n_p,)), dma((n_p,)),
            dma((n_p,)), dma((n_p,)),
            dma((n_p,)), dma((n_p,)),
            dma((n_c,)), dma((n_c,)),
            dma(()), dma(()),
            dma((n_q,)), dma((n_q,)),
            dma((n_q,)), dma((n_q,)),
            dma((n_q,)), dma((n_q,)),
        ],
        compiler_params=pltpu.CompilerParams(
            collective_id=0, has_side_effects=True, vmem_limit_bytes=60 * 1024 * 1024
        ),
    )(tile_count, tile_rows, sketch_pick, block_targets, points, weights, core_inv)
    grad = slab + rest
    return grad, grad - fix


def solution(mesh):
    in_specs = (
        P(("grp", "pts", "sub"), None),
        P(("grp", "pts", "sub"), None),
        P(("grp", "col"), ("pts", "sub"), None),
        P(("grp", "col"), None),
        P(("grp", "col"), None),
        P(("grp", "col"), ("pts", "sub"), None),
        P("grp", None),
    )
    out_specs = (P(("grp", "col"), ("pts", "sub"), None), P(("grp", "col"), ("pts", "sub"), None))
    mesh_sizes = (mesh.shape["pts"], mesh.shape["col"], mesh.shape["sub"])
    return jax.shard_map(
        functools.partial(per_device, mesh_sizes), mesh=mesh, in_specs=in_specs,
        out_specs=out_specs, check_vma=False,
    )
```

```python
import functools
import math

import jax
import jax.numpy as jnp
from jax import lax
from jax.experimental import pallas as pl
from jax.experimental.pallas import tpu as pltpu
from jax.sharding import PartitionSpec as P

RIDGE_COEF = 50.0
MESH = pl.DeviceIdType.MESH
F32 = jnp.float32
BF16 = jnp.bfloat16
NN = (((1,), (0,)), ((), ()))
NT = (((1,), (1,)), ((), ()))


def mm(left, right, dims=NN):
    return lax.dot_general(left, right, dims, preferred_element_type=F32)


def split2(value):
    high = value.astype(BF16)
    return high, (value - high.astype(F32)).astype(BF16)


def mm3(left, right, dims=NN):
    (lh, ll), (rh, rl) = left, right
    return mm(lh, rh, dims) + (mm(lh, rl, dims) + mm(ll, rh, dims))


def mix(index, step, total):
    if total & (total - 1):
        return (index + step) % total
    out, bit = 0, 1
    while bit < total:
        out = out + bit * (((index // bit) % 2 + (step // bit) % 2) % 2)
        bit *= 2
    return out


def each(low, high, body):
    if high - low <= 8:
        for i in range(low, high):
            body(i)
    elif high > low:
        lax.fori_loop(low, high, lambda i, c: (body(i), c)[1], 0)


def sq_col(x):
    wide = x.astype(F32)
    return jnp.sum(wide * wide, axis=1, keepdims=True)


def sq_row(x):
    wide = x.astype(F32)
    high, low = split2(wide * wide)
    ones = jnp.ones((8, x.shape[1]), BF16)
    return (mm(ones, high, NT) + mm(ones, low, NT))[0:1, :]


def column(row):
    return jnp.transpose(jnp.broadcast_to(row, (8, row.shape[1])))[:, 0:1]


def body(
    sizes, cnt_hbm, rows_hbm, pick_hbm, targ_hbm, points_hbm, weights_hbm, core_hbm,
    slab_ref, rest_ref, fix_ref,
    cnt_ref, rows_ref, pick_ref, targ_ref,
    pts_v, wts_v, core_v, psq, core_hi, core_lo,
    xbuf, part, subr, lsum, lrec, skx, out_hi, out_lo, gbuf, psum, prec, fbuf,
    in_sem, ag_s, ag_r, fw_s, fw_r, sb_s, sb_r, ln_s, ln_r, sk_s, sk_r,
    pe_s, pe_r, rs_s, rs_r, fa_s, fa_r, ff_s, ff_r,
):
    n_p, n_c, n_s, cap, width, outs, n_pts, n_sk, rank, piece = sizes
    n_q = n_p * n_c
    half = rank // n_s
    owners = n_p * n_s
    p = lax.axis_index("pts")
    c = lax.axis_index("col")
    s = lax.axis_index("sub")
    q = p * n_c + c
    other = 1 - s
    sibling = {"sub": other}
    c2 = math.log2(math.e) / width

    def at_q(k):
        peer = mix(q, k, n_q)
        return peer, {"pts": peer // n_c, "col": peer % n_c}

    def rc(src, dst, ssem, rsem, dev):
        return pltpu.make_async_remote_copy(
            src_ref=src, dst_ref=dst, send_sem=ssem, recv_sem=rsem,
            device_id=dev, device_id_type=MESH,
        )

    loads = [
        pltpu.make_async_copy(src, dst, in_sem.at[i])
        for i, (src, dst) in enumerate((
            (cnt_hbm, cnt_ref), (rows_hbm, rows_ref), (points_hbm, pts_v), (weights_hbm, wts_v),
            (pick_hbm, pick_ref), (targ_hbm, targ_ref), (core_hbm, core_v),
        ))
    ]
    for load in loads:
        load.start()
    in_cnt, in_rows, in_pts, in_wts, in_pick, in_targ, in_core = loads

    barrier = pltpu.get_barrier_semaphore()
    pl.semaphore_signal(barrier, inc=1, device_id=sibling, device_id_type=MESH)

    def greet(dev):
        pl.semaphore_signal(barrier, inc=1, device_id=dev, device_id_type=MESH)

    each(1, n_p, lambda k: greet({"pts": mix(p, k, n_p)}))
    each(1, n_c, lambda k: greet({"col": mix(c, k, n_c)}))

    in_cnt.wait()
    in_rows.wait()
    own_count = cnt_ref[0, p * n_s + s]
    used = lax.broadcasted_iota(jnp.int32, (cap, 1), 0) < own_count
    rows = jnp.where(used, column(rows_ref[0].astype(F32)), -1.0)
    ids = lax.broadcasted_iota(jnp.int32, (1, n_pts), 1).astype(F32)
    pick_rows = jnp.where(rows == ids, 1.0, 0.0).astype(BF16)
    in_pts.wait()
    xbuf[p, s] = mm(pick_rows, pts_v[...]).astype(BF16)
    pl.semaphore_wait(barrier, n_p + n_c - 1)

    def fw(pk, slot):
        return rc(xbuf.at[pk, slot], xbuf.at[pk, slot], fw_s.at[pk], fw_r.at[pk], sibling)

    fw(p, s).start()

    def ag_send(k):
        peer = mix(p, k, n_p)
        rc(xbuf.at[p, s], xbuf.at[p, s], ag_s.at[peer], ag_r.at[p], {"pts": peer}).start()

    each(1, n_p, ag_send)

    in_wts.wait()
    alpha = mm(pick_rows, wts_v[...])
    psq[...] = sq_row(pts_v[...]) * c2

    def lane_forward(k):
        pk = mix(p, k, n_p)
        rc(xbuf.at[pk, s], xbuf.at[pk, s], ag_s.at[pk], ag_r.at[pk], {"pts": pk}).wait_recv()
        fw(pk, s).start()

    step = math.gcd(n_pts, 512)

    def compute(k):
        pk = mix(p, k, n_p)
        fw(pk, other).wait_recv()
        x = xbuf[pk].reshape(n_s * cap, width)
        left = sq_col(x) * c2

        acc = jnp.zeros((n_s * cap, outs), F32)
        for i in range(n_pts // step):
            at = slice(i * step, (i + 1) * step)
            inner = mm(x, pts_v[at, :], NT)
            vals = jnp.exp2((inner * (2.0 * c2) - left) - psq[:, at])
            high, low = split2(vals)
            w = wts_v[at, :]
            acc = acc + (mm(high, w) + mm(low, w))
        part[pk] = acc.reshape(n_s, cap, outs)
        rc(part.at[pk, other], subr.at[pk], sb_s.at[pk], sb_r.at[pk], sibling).start()

    def sub_wait(pk):
        rc(part.at[pk, other], subr.at[pk], sb_s.at[pk], sb_r.at[pk], sibling).wait_recv()

    def lane_send(k):
        pk = mix(p, k, n_p)
        sub_wait(pk)
        lsum[pk] = part[pk, s] + subr[pk]
        rc(lsum.at[pk], lrec.at[p], ln_s.at[pk], ln_r.at[p], {"pts": pk}).start()

    compute(0)
    if n_p > 1:
        lane_forward(1)

        def stage(k):
            lane_forward(k + 1)
            compute(k)

            @pl.when(k >= 2)
            def _():
                lane_send(k - 1)

        if n_p <= 4:
            for k in range(1, n_p - 1):
                lane_forward(k + 1)
                compute(k)
                if k >= 2:
                    lane_send(k - 1)
        else:
            lax.fori_loop(1, n_p - 1, lambda k, z: (stage(k), z)[1], 0)
        compute(n_p - 1)
        if n_p > 2:
            lane_send(n_p - 2)

    slot = lax.broadcasted_iota(jnp.int32, (1, owners * cap), 1)
    rank_of = jnp.full((1, owners * cap), -1, jnp.int32)
    before = 0
    for o in range(owners):
        have = cnt_ref[0, o]
        local = slot - o * cap
        rank_of = jnp.where((local >= 0) & (local < have), local + before, rank_of)
        before = before + have
    in_pick.wait()
    picks = column(pick_ref[...].astype(F32))
    onehot = jnp.where(picks == rank_of.astype(F32), 1.0, 0.0).astype(BF16)
    def rows_of(k):
        return pl.ds(pl.multiple_of(k * n_sk, n_sk), n_sk)

    skx[rows_of(c), :] = mm(onehot, xbuf[...].reshape(owners * cap, width)).astype(BF16)

    def sk(ck, mine):
        at = skx.at[rows_of(mine), :]
        return rc(at, at, sk_s.at[ck], sk_r.at[mine], {"col": ck})

    each(1, n_c, lambda k: sk(mix(c, k, n_c), c).start())
    if n_p > 1:
        lane_send(n_p - 1)

    in_core.wait()
    high, low = split2(core_v[...])
    core_hi[...] = high
    core_lo[...] = low

    each(1, n_c, lambda k: sk(mix(c, k, n_c), mix(c, k, n_c)).wait_recv())
    own_x = xbuf[p, s]
    sketch = skx[...]
    pair_x = xbuf[p].reshape(n_s * cap, width)
    mine_x = skx[pl.ds(pl.multiple_of(s * half, half), half), :]
    kern_t = jnp.exp2((mm(mine_x, pair_x, NT) * (2.0 * c2) - sq_col(mine_x) * c2) - sq_row(pair_x) * c2)
    kern_t = split2(kern_t)
    kern = jnp.exp2((mm(own_x, sketch, NT) * (2.0 * c2) - sq_col(own_x) * c2) - sq_row(sketch) * c2)
    high, low = split2(mm3(split2(kern), (core_hi[...], core_lo[...])))
    out_hi[...] = high
    out_lo[...] = low

    sub_wait(p)
    slab = part[p, s] + subr[p]
    for k in range(1, n_p):
        pk = mix(p, k, n_p)
        rc(lsum.at[pk], lrec.at[pk], ln_s.at[pk], ln_r.at[pk], {"pts": pk}).wait_recv()
        slab = slab + lrec[pk]
    in_targ.wait()
    used_f = used.astype(F32)
    rest = used_f * (RIDGE_COEF * alpha - targ_ref[0].astype(F32))
    slab = used_f * slab
    slab_ref[0] = slab
    rest_ref[0] = rest
    grad = slab + rest

    gbuf[s] = grad
    pe = rc(gbuf.at[s], gbuf.at[s], pe_s, pe_r, sibling)
    pe.start()
    rc(gbuf.at[other], gbuf.at[other], pe_s, pe_r, sibling).wait_recv()
    proj = mm3(kern_t, split2(gbuf[...].reshape(n_s * cap, outs)))
    if half < n_q * piece:
        proj = jnp.concatenate([proj, jnp.zeros((n_q * piece - half, outs), F32)], axis=0)
    psum[...] = proj.reshape(n_q, piece, outs)

    def rs(k, mine):
        peer, dev = at_q(k)
        return rc(psum.at[peer], prec.at[mine(peer)], rs_s.at[peer], rs_r.at[mine(peer)], dev)

    each(1, n_q, lambda k: rs(k, lambda peer: q).start())
    total = psum[q]
    if n_q <= 8:
        for k in range(1, n_q):
            rs(k, lambda peer: peer).wait_recv()
            total = total + prec[mix(q, k, n_q)]
    else:
        def gain(k, run):
            rs(k, lambda peer: peer).wait_recv()
            return run + prec[mix(q, k, n_q)]

        total = lax.fori_loop(1, n_q, gain, total)
    fbuf[s, q] = total

    def fa(k, mine):
        peer, dev = at_q(k)
        at = fbuf.at[s, mine(peer)]
        return rc(at, at, fa_s.at[peer], fa_r.at[mine(peer)], dev)

    def ff(peer, side):
        at = fbuf.at[side, peer]
        return rc(at, at, ff_s.at[peer], ff_r.at[peer], sibling)

    each(1, n_q, lambda k: fa(k, lambda peer: q).start())
    ff(q, s).start()

    def relay(k):
        fa(k, lambda peer: peer).wait_recv()
        ff(mix(q, k, n_q), s).start()

    each(1, n_q, relay)

    def correct(h):
        block = fbuf[h].reshape(n_q * piece, outs)[0:half, :]
        cols = pl.ds(pl.multiple_of(h * half, half), half)
        return mm3((out_hi[:, cols], out_lo[:, cols]), split2(block))

    fix = correct(s)
    each(0, n_q, lambda k: ff(mix(q, k, n_q), other).wait_recv())
    fix_ref[0] = used_f * (fix + correct(other))

    def lane_done(k):
        pk = mix(p, k, n_p)
        rc(xbuf.at[p, s], xbuf.at[p, s], ag_s.at[pk], ag_r.at[p], {"pts": pk}).wait_send()
        rc(lsum.at[pk], lrec.at[p], ln_s.at[pk], ln_r.at[p], {"pts": pk}).wait_send()

    def chip_done(k):
        pk = mix(p, k, n_p)
        fw(pk, s).wait_send()
        rc(part.at[pk, other], subr.at[pk], sb_s.at[pk], sb_r.at[pk], sibling).wait_send()

    def piece_done(k):
        rs(k, lambda peer: q).wait_send()
        fa(k, lambda peer: q).wait_send()

    each(1, n_p, lane_done)
    each(0, n_p, chip_done)
    each(1, n_c, lambda k: sk(mix(c, k, n_c), c).wait_send())
    pe.wait_send()
    each(1, n_q, piece_done)
    each(0, n_q, lambda k: ff(mix(q, k, n_q), s).wait_send())


def per_device(mesh_sizes, points, weights, tile_rows, tile_count, sketch_pick, block_targets, core_inv):
    n_p, n_c, n_s = mesh_sizes
    cap = tile_rows.shape[2]
    n_pts, width = points.shape
    outs = weights.shape[1]
    n_sk = sketch_pick.shape[1]
    rank = core_inv.shape[0]
    n_q = n_p * n_c
    piece = max(8, -(-rank // (n_s * n_q)))
    sizes = (n_p, n_c, n_s, cap, width, outs, n_pts, n_sk, rank, piece)
    vmem = pl.BlockSpec(memory_space=pltpu.VMEM)
    hbm = pl.BlockSpec(memory_space=pl.ANY)
    dma = pltpu.SemaphoreType.DMA
    out = jax.ShapeDtypeStruct((1, cap, outs), F32)
    slab, rest, fix = pl.pallas_call(
        functools.partial(body, sizes),
        out_shape=(out, out, out),
        in_specs=[hbm] * 7,
        out_specs=(vmem, vmem, vmem),
        scratch_shapes=[
            pltpu.SMEM(tile_count.shape, jnp.int32),
            pltpu.VMEM(tile_rows.shape, jnp.int32),
            pltpu.VMEM(sketch_pick.shape, jnp.int32),
            pltpu.VMEM(block_targets.shape, BF16),
            pltpu.VMEM((n_pts, width), BF16),
            pltpu.VMEM((n_pts, outs), BF16),
            pltpu.VMEM((rank, rank), F32),
            pltpu.VMEM((1, n_pts), F32),
            pltpu.VMEM((rank, rank), BF16),
            pltpu.VMEM((rank, rank), BF16),
            pltpu.VMEM((n_p, n_s, cap, width), BF16),
            pltpu.VMEM((n_p, n_s, cap, outs), F32),
            pltpu.VMEM((n_p, cap, outs), F32),
            pltpu.VMEM((n_p, cap, outs), F32),
            pltpu.VMEM((n_p, cap, outs), F32),
            pltpu.VMEM((n_c * n_sk, width), BF16),
            pltpu.VMEM((cap, rank), BF16),
            pltpu.VMEM((cap, rank), BF16),
            pltpu.VMEM((n_s, cap, outs), F32),
            pltpu.VMEM((n_q, piece, outs), F32),
            pltpu.VMEM((n_q, piece, outs), F32),
            pltpu.VMEM((n_s, n_q, piece, outs), F32),
            dma((7,)),
            dma((n_p,)), dma((n_p,)),
            dma((n_p,)), dma((n_p,)),
            dma((n_p,)), dma((n_p,)),
            dma((n_p,)), dma((n_p,)),
            dma((n_c,)), dma((n_c,)),
            dma(()), dma(()),
            dma((n_q,)), dma((n_q,)),
            dma((n_q,)), dma((n_q,)),
            dma((n_q,)), dma((n_q,)),
        ],
        compiler_params=pltpu.CompilerParams(
            collective_id=0, has_side_effects=True, vmem_limit_bytes=60 * 1024 * 1024
        ),
    )(tile_count, tile_rows, sketch_pick, block_targets, points, weights, core_inv)
    grad = slab + rest
    return grad, grad - fix


def solution(mesh):
    in_specs = (
        P(("grp", "pts", "sub"), None),
        P(("grp", "pts", "sub"), None),
        P(("grp", "col"), ("pts", "sub"), None),
        P(("grp", "col"), None),
        P(("grp", "col"), None),
        P(("grp", "col"), ("pts", "sub"), None),
        P("grp", None),
    )
    out_specs = (P(("grp", "col"), ("pts", "sub"), None), P(("grp", "col"), ("pts", "sub"), None))
    mesh_sizes = (mesh.shape["pts"], mesh.shape["col"], mesh.shape["sub"])
    return jax.shard_map(
        functools.partial(per_device, mesh_sizes), mesh=mesh, in_specs=in_specs,
        out_specs=out_specs, check_vma=False,
    )
```
